512 devices in a mesh: row: 32 (over x, y), col: 16 (over z, core).
Axes of the slice: x: 4, y: 8, z: 8, core: 2. Of those that a mesh axis runs over, the one named last changes fastest.
Arguments:
- matrix: float32 [1, 4096, 2, 2048], P(None, 'row', None, 'col'), may hold values from 0 to 2, as said below
Outputs:
- factored: float32 [1, 4096, 2, 2048], P(None, 'row', None, 'col')
The draws below stay inside these ranges and needn't reach their ends.
Inputs may be any that keep to these rules, and one draw needn't show every extreme that they name: `matrix`: symmetric and positive definite, with every eigenvalue at least 1.
All inputs are finite; a program needn't handle non-finite values.
Results may differ from the reference program's by a relative error of at most 0.0003.
Values sent between devices are 32-bit elements; how exact they have to be, the bound alone decides.
No kernel may reach another device: no remote copies, remote signals or barrier semaphores. Data moves between devices by JAX's collectives and lax.ppermute only.
A program may use at most 64 MiB of HBM per device.

```python
import jax
import jax.numpy as jnp
from jax import lax

TILE = 128
PANEL = 384
TR = 1
ROW_SPAN = 4096
COL_SPAN = 2048
ORDER = 4096
TC = 2
N_ROW = 32


def draw_matrix(key, part):
    key = jax.random.fold_in(key, 7)
    point_key = jax.random.fold_in(key, 0)
    points = jax.random.normal(point_key, (ORDER, 16), jnp.float32)
    distance = jnp.zeros((ORDER, ORDER), jnp.float32)
    for feature in range(16):
        column = points[:, feature]
        distance = distance + (column[:, None] - column[None, :]) ** 2
    kernel = jnp.exp(-distance / 16.0) + jnp.eye(ORDER, dtype=jnp.float32)
    return kernel.reshape(TR, ROW_SPAN, TC, COL_SPAN)


def setup_inputs(seed: int = 0) -> dict:
    key_list = jax.random.split(jax.random.key(seed), 2)
    matrix = draw_matrix(jax.random.fold_in(key_list[1], 71), 0)
    return dict(matrix=matrix)


def panel_step(current, panel_start, panel_width):
    matrix_order = current.shape[0]
    panel_end = panel_start + panel_width
    panel_cols = current[:, panel_start:panel_end]
    diag_block = panel_cols[panel_start:panel_end]
    diag_factor = jnp.linalg.cholesky(diag_block)
    identity = jnp.eye(panel_width, dtype=current.dtype)
    inverse_factor = jax.scipy.linalg.solve_triangular(diag_factor, identity, lower=True)
    product = jnp.dot(panel_cols, inverse_factor.T, precision=lax.Precision.HIGHEST)
    row_index = jnp.arange(matrix_order, dtype=jnp.int32)[:, None]
    col_index = panel_start + jnp.arange(panel_width, dtype=jnp.int32)[None, :]
    panel = jnp.where(row_index >= col_index, product, jnp.zeros_like(product))
    below_rows = panel[panel_end:]
    current = current.at[panel_end:, panel_end:].add(-jnp.dot(below_rows, below_rows.T, precision=lax.Precision.HIGHEST))
    current = current.at[panel_start:panel_end, panel_end:].set(0.0)
    current = current.at[:, panel_start:panel_end].set(panel)
    return current

def reference(matrix):
    matrix_order = TR * N_ROW * TILE
    current = matrix.reshape(matrix_order, matrix_order)
    for panel_start in (0, PANEL):
        current = panel_step(current, panel_start, PANEL)
    return current.reshape(matrix.shape)
```

```python
import jax
import jax.numpy as jnp
from jax import lax
from jax.experimental import pallas as pl
from jax.experimental.pallas import tpu as pltpu
from jax.sharding import PartitionSpec as P

TILE = 128
NB = 6
GROUP = 32
XS, YS, ZS = 4, 8, 8
ZSRC = NB // 2
PAYLOAD = 5
VMEM_LIMIT = 48 * 1024 * 1024
HI = lax.Precision.HIGHEST


def dot(a, b):
    return lax.dot_general(a, b, (((1,), (0,)), ((), ())), precision=HI, preferred_element_type=jnp.float32)


def dot_t(a, b):
    return lax.dot_general(a, b, (((0,), (0,)), ((), ())), precision=HI, preferred_element_type=jnp.float32)


def spread(row):
    return jnp.broadcast_to(row, (8, row.shape[1]))


def eliminate(rows, offset):
    count, width = rows.shape
    groups = count // 8
    wide = width // TILE
    block = rows[:, offset : offset + count]
    column = {}
    for j in range(count):
        for g in range(j // 8, groups):
            column[g, j] = jnp.broadcast_to(block[8 * g : 8 * g + 8, j : j + 1], (8, TILE))
    part = [rows[8 * g : 8 * g + 8] for g in range(groups)]
    sublane = lax.broadcasted_iota(jnp.int32, (8, TILE), 0)
    scale = [None] * groups
    for k in range(count):
        gk, sk = divmod(k, 8)
        pivot = spread(column[gk, k][sk : sk + 1])
        inverse = pl.reciprocal(pivot)
        root = lax.rsqrt(pivot)
        scale[gk] = root if scale[gk] is None else jnp.where(sublane == sk, root, scale[gk])
        factor = {}
        for g in range(gk, groups):
            value = column[g, k] * inverse
            factor[g] = jnp.where(sublane > sk, value, 0.0) if g == gk else value
        for j in range(k + 1, count):
            gj, sj = divmod(j, 8)
            across = spread(column[gj, k][sj : sj + 1])
            for g in range(gj, groups):
                column[g, j] = column[g, j] - factor[g] * across
        pivot_row = spread(part[gk][sk : sk + 1])
        for g in range(gk, groups):
            if g == gk and sk == 7:
                continue
            part[g] = part[g] - jnp.concatenate([factor[g]] * wide, axis=1) * pivot_row
    return jnp.concatenate(
        [part[g] * jnp.concatenate([scale[g]] * wide, axis=1) for g in range(groups)], axis=0
    )


def factor_tile(tile):
    row = lax.broadcasted_iota(jnp.int32, (TILE, TILE), 0)
    lane = lax.broadcasted_iota(jnp.int32, (TILE, TILE), 1)
    both = jnp.concatenate([tile, jnp.where(row == lane, 1.0, 0.0)], axis=1)
    upper = None
    for start in range(0, TILE, GROUP):
        rows = both[start : start + GROUP]
        if upper is not None:
            rows = rows - dot_t(upper[:, start : start + GROUP], upper)
        rows = eliminate(rows, start)
        upper = rows if upper is None else jnp.concatenate([upper, rows], axis=0)
    return upper[:, :TILE], upper[:, TILE:]


def pick_kernel(place, *refs):
    sources, out = refs[:-1], refs[-1]
    for j in range(out.shape[0]):
        for s in range(len(sources)):

            @pl.when(place[j] == s)
            def _():
                out[j] = sources[s][...]


def pick(place, arrays, count):
    shape = arrays[0].shape
    return pl.pallas_call(
        pick_kernel,
        out_shape=jax.ShapeDtypeStruct((count,) + shape, jnp.float32),
        in_specs=[pl.BlockSpec(memory_space=pltpu.SMEM)]
        + [pl.BlockSpec(memory_space=pltpu.VMEM)] * len(arrays),
        out_specs=pl.BlockSpec(memory_space=pltpu.VMEM),
        compiler_params=pltpu.CompilerParams(vmem_limit_bytes=VMEM_LIMIT),
    )(place, *arrays)


def panels_kernel(place, mine, strip, near, far, out, work):
    row_tile, col_tile, core = place[0], place[1], place[2]
    width = work.shape[1]
    right = NB * TILE
    for i in range(NB):
        work[i * TILE : (i + 1) * TILE, right : right + 2 * TILE] = strip[i]

    def place_tiles(source, parity):
        for z in range(ZSRC):
            j = 2 * z + parity
            for t in range(PAYLOAD - 1):
                i = (j + t) % NB
                if t == NB // 2 and j >= NB // 2:
                    continue
                tile = source[z, t * TILE : (t + 1) * TILE, :]
                if i <= j:
                    work[i * TILE : (i + 1) * TILE, j * TILE : (j + 1) * TILE] = tile
                else:
                    work[j * TILE : (j + 1) * TILE, i * TILE : (i + 1) * TILE] = tile.T
            tile = source[z, (PAYLOAD - 1) * TILE :, :]
            work[j * TILE : (j + 1) * TILE, right + 2 * TILE :] = tile.T

    for parity in range(2):

        @pl.when(core == parity)
        def _():
            place_tiles(near, parity)

        @pl.when(core != parity)
        def _():
            place_tiles(far, parity)

    for b in range(NB):
        lo, hi = b * TILE, (b + 1) * TILE
        rows = work[lo:hi, lo:]
        if b:
            rows = rows - dot_t(work[:lo, lo:hi], work[:lo, lo:])
        upper, inverse = factor_tile(rows[:, :TILE])
        work[lo:hi, lo:hi] = upper
        work[lo:hi, hi:] = dot(inverse, rows[:, TILE:])

    mine_row = work[:, right + 2 * TILE :]
    trailing = mine[...] - dot_t(mine_row, work[:, right : right + 2 * TILE])
    out[...] = jnp.where(row_tile >= NB, trailing, 0.0)
    row = lax.broadcasted_iota(jnp.int32, (TILE, TILE), 0)
    lane = lax.broadcasted_iota(jnp.int32, (TILE, TILE), 1)
    for j in range(NB):

        @pl.when(col_tile == j)
        def _():
            tile = work[j * TILE : (j + 1) * TILE, right + 2 * TILE :].T
            keep = row + (row_tile - j) * TILE >= lane
            out[:, :TILE] = jnp.where(keep, tile, 0.0)


def send(array, pairs):
    return lax.ppermute(array, ("row", "col"), pairs)


def device(x, y, z, core):
    return ((x % XS) * YS + y % YS) * (2 * ZS) + (z % ZS) * 2 + core


def per_device(matrix):
    block = matrix.reshape(matrix.shape[1], matrix.shape[2] * matrix.shape[3])
    row_tile = lax.axis_index("row")
    col_tile = lax.axis_index("col")
    x, y = row_tile // YS, row_tile % YS
    z, core = col_tile // 2, col_tile % 2
    columns = [(zz, cc) for zz in range(ZS) for cc in range(2)]
    chips = [(xx, yy) for xx in range(XS) for yy in range(YS)]

    pieces = block
    for step in range(1, XS):
        pairs = [
            (device(0, yy, *col), device(step, yy, *col)) for yy in range(NB) for col in columns
        ]
        arrived = send(block, pairs)
        pieces = jnp.where(x == step, arrived, pieces)
    held = [pieces]
    for step in range(1, YS):
        pairs = [
            (device(xx, yy, *col), device(xx, yy + step, *col))
            for xx in range(XS)
            for yy in range(NB)
            for col in columns
        ]
        held.append(send(pieces, pairs))
    strip = pick((y - jnp.arange(NB, dtype=jnp.int32)) % YS, held, NB)

    first = strip[:, :, :TILE].reshape(NB * TILE, TILE)
    twice = jnp.concatenate([first, first], axis=0)
    start = jnp.minimum(col_tile, NB) * TILE
    payload = jnp.concatenate(
        [
            lax.dynamic_slice_in_dim(twice, start, (PAYLOAD - 1) * TILE, 0),
            block[:, :TILE],
        ],
        axis=0,
    )
    held = [payload]
    for step in range(1, ZS):
        pairs = [
            (device(*chip, zz, cc), device(*chip, zz + step, cc))
            for chip in chips
            for zz in range(ZSRC)
            for cc in range(2)
        ]
        held.append(send(payload, pairs))
    near = pick((z - jnp.arange(ZSRC, dtype=jnp.int32)) % ZS, held, ZSRC)
    pairs = [
        (device(*chip, zz, cc), device(*chip, zz, 1 - cc))
        for chip in chips
        for zz, cc in columns
    ]
    far = send(near, pairs)

    place = jnp.stack([row_tile, col_tile, core]).astype(jnp.int32)
    vmem = pl.BlockSpec(memory_space=pltpu.VMEM)
    result = pl.pallas_call(
        panels_kernel,
        out_shape=jax.ShapeDtypeStruct(block.shape, jnp.float32),
        in_specs=[pl.BlockSpec(memory_space=pltpu.SMEM), vmem, vmem, vmem, vmem],
        out_specs=vmem,
        scratch_shapes=[pltpu.VMEM((NB * TILE, (NB + 3) * TILE), jnp.float32)],
        compiler_params=pltpu.CompilerParams(vmem_limit_bytes=VMEM_LIMIT),
    )(place, block, strip, near, far)
    return result.reshape(matrix.shape)


def solution(mesh):
    placed = (P(None, "row", None, "col"),)
    return jax.shard_map(
        per_device,
        mesh=mesh,
        in_specs=placed,
        out_specs=P(None, "row", None, "col"),
        check_vma=False,
    )
```

```python
import jax
import jax.numpy as jnp
from jax import lax
from jax.experimental import pallas as pl
from jax.experimental.pallas import tpu as pltpu
from jax.sharding import PartitionSpec as P

TILE = 128
NB = 6
GROUP = 32
XS, YS, ZS = 4, 8, 8
ZSRC = NB // 2
VMEM_LIMIT = 48 * 1024 * 1024
HI = lax.Precision.HIGHEST


def dot(a, b):
    return lax.dot_general(a, b, (((1,), (0,)), ((), ())), precision=HI, preferred_element_type=jnp.float32)


def dot_t(a, b):
    return lax.dot_general(a, b, (((0,), (0,)), ((), ())), precision=HI, preferred_element_type=jnp.float32)


def spread(row):
    return jnp.broadcast_to(row, (8, row.shape[1]))


def eliminate(rows, offset):
    count, width = rows.shape
    groups = count // 8
    wide = width // TILE
    block = rows[:, offset : offset + count]
    column = {}
    for j in range(count):
        for g in range(j // 8, groups):
            column[g, j] = jnp.broadcast_to(block[8 * g : 8 * g + 8, j : j + 1], (8, TILE))
    part = [rows[8 * g : 8 * g + 8] for g in range(groups)]
    sublane = lax.broadcasted_iota(jnp.int32, (8, TILE), 0)
    scale = [None] * groups
    for k in range(count):
        gk, sk = divmod(k, 8)
        pivot = spread(column[gk, k][sk : sk + 1])
        inverse = pl.reciprocal(pivot)
        root = lax.rsqrt(pivot)
        scale[gk] = root if scale[gk] is None else jnp.where(sublane == sk, root, scale[gk])
        factor = {}
        for g in range(gk, groups):
            value = column[g, k] * inverse
            factor[g] = jnp.where(sublane > sk, value, 0.0) if g == gk else value
        for j in range(k + 1, count):
            gj, sj = divmod(j, 8)
            across = spread(column[gj, k][sj : sj + 1])
            for g in range(gj, groups):
                column[g, j] = column[g, j] - factor[g] * across
        pivot_row = spread(part[gk][sk : sk + 1])
        for g in range(gk, groups):
            if g == gk and sk == 7:
                continue
            part[g] = part[g] - jnp.concatenate([factor[g]] * wide, axis=1) * pivot_row
    return jnp.concatenate(
        [part[g] * jnp.concatenate([scale[g]] * wide, axis=1) for g in range(groups)], axis=0
    )


def factor_tile(tile):
    row = lax.broadcasted_iota(jnp.int32, (TILE, TILE), 0)
    lane = lax.broadcasted_iota(jnp.int32, (TILE, TILE), 1)
    both = jnp.concatenate([tile, jnp.where(row == lane, 1.0, 0.0)], axis=1)
    upper = None
    for start in range(0, TILE, GROUP):
        rows = both[start : start + GROUP]
        if upper is not None:
            rows = rows - dot_t(upper[:, start : start + GROUP], upper)
        rows = eliminate(rows, start)
        upper = rows if upper is None else jnp.concatenate([upper, rows], axis=0)
    return upper[:, :TILE], upper[:, TILE:]


def dot_nt(a, b):
    return lax.dot_general(a, b, (((1,), (1,)), ((), ())), precision=HI, preferred_element_type=jnp.float32)


def factor_kernel(place, near, far, inverse, upper):
    core = place[2]

    def place_tiles(source, shift):
        for i in range(NB):
            if (i + shift) % 2 != place_tiles.parity:
                continue
            for half in range(2):
                distance = shift + 2 * half
                j = (i + distance) % NB
                if distance == NB // 2 and i >= NB // 2:
                    continue
                tile = source[i, half * TILE : (half + 1) * TILE, :]
                if i <= j:
                    upper[i * TILE : (i + 1) * TILE, j * TILE : (j + 1) * TILE] = tile
                else:
                    upper[j * TILE : (j + 1) * TILE, i * TILE : (i + 1) * TILE] = tile.T

    for parity in range(2):

        @pl.when(core == parity)
        def _():
            for source, held in ((near, parity), (far, 1 - parity)):
                place_tiles.parity = held
                place_tiles(source, 0)
                place_tiles(source, 1)

    for b in range(NB):
        lo, hi = b * TILE, (b + 1) * TILE
        rows = upper[lo:hi, lo:]
        if b:
            rows = rows - dot_t(upper[:lo, lo:hi], upper[:lo, lo:])
        _, own = factor_tile(rows[:, :TILE])
        inverse[lo:hi, lo:hi] = own
        if hi < NB * TILE:
            upper[lo:hi, hi:] = dot(own, rows[:, TILE:])
            inverse[lo:hi, hi:] = jnp.zeros((TILE, NB * TILE - hi), jnp.float32)
        if b:
            inverse[lo:hi, :lo] = -dot(own, dot_t(upper[:lo, lo:hi], inverse[:lo, :lo]))


def update_kernel(place, mine, strip, near, far, inverse, out, row_strip, solved):
    row_tile, col_tile, core = place[0], place[1], place[2]

    for parity in range(2):

        @pl.when(core == parity)
        def _():
            for j in range(NB):
                source = near if j % 2 == parity else far
                row_strip[:, j * TILE : (j + 1) * TILE] = source[j // 2]

    panel = []
    for b in range(NB):
        hi = (b + 1) * TILE
        lower = inverse[b * TILE : hi, :hi]
        total = None
        for i in range(b + 1):
            term = dot(lower[:, i * TILE : (i + 1) * TILE], strip[i])
            total = term if total is None else total + term
        solved[b * TILE : hi, :] = total
        panel.append(dot_nt(row_strip[:, :hi], lower))
    trailing = mine[...] - dot(jnp.concatenate(panel, axis=1), solved[...])
    out[...] = jnp.where(row_tile >= NB, trailing, 0.0)
    row = lax.broadcasted_iota(jnp.int32, (TILE, TILE), 0)
    lane = lax.broadcasted_iota(jnp.int32, (TILE, TILE), 1)
    for j in range(NB):

        @pl.when(col_tile == j)
        def _():
            keep = row + (row_tile - j) * TILE >= lane
            out[:, :TILE] = jnp.where(keep, panel[j], 0.0)


def send(array, pairs):
    return lax.ppermute(array, ("row", "col"), pairs)


def device(x, y, z, core):
    return ((x % XS) * YS + y % YS) * (2 * ZS) + (z % ZS) * 2 + core


CHIPS = [(x, y) for x in range(XS) for y in range(YS)]
COLUMNS = [(z, core) for z in range(ZS) for core in range(2)]
Y_GROUPS = [[x * YS + y for y in range(YS)] for x in range(XS)]
Z_GROUPS = [[z * 2 + core for z in range(ZS)] for core in range(2)]


def along_x(array, x):
    result = array
    for step in range(1, XS):
        pairs = [(device(0, y, *col), device(step, y, *col)) for y in range(NB) for col in COLUMNS]
        result = jnp.where(x == step, send(array, pairs), result)
    return result


def to_all(array, axis, groups):
    copies = jnp.broadcast_to(array, (len(groups[0]),) + array.shape)
    return lax.all_to_all(copies, axis, 0, 0, axis_index_groups=groups)


def per_device(matrix):
    block = matrix.reshape(matrix.shape[1], matrix.shape[2] * matrix.shape[3])
    row_tile = lax.axis_index("row")
    col_tile = lax.axis_index("col")
    x = row_tile // YS
    core = col_tile % 2

    strip = lax.all_gather(along_x(block, x), "row", axis_index_groups=Y_GROUPS)

    near_row = to_all(block[:, :TILE], "col", Z_GROUPS)[:ZSRC]

    first = jnp.where(row_tile % 2 == core, row_tile, (row_tile + 1) % NB)
    start = jnp.clip((first - core) // 2, 0, ZSRC - 1)
    wrapped = jnp.concatenate([near_row, near_row[:1]], axis=0)
    tiles = lax.dynamic_slice_in_dim(wrapped, start, 2, 0).reshape(2 * TILE, TILE)
    near = to_all(along_x(tiles, x), "row", Y_GROUPS)[:NB]

    swap = [(device(*chip, z, c), device(*chip, z, 1 - c)) for chip in CHIPS for z, c in COLUMNS]
    far = send(near, swap)
    far_row = send(near_row, swap)

    place = jnp.stack([row_tile, col_tile, core]).astype(jnp.int32)
    smem = pl.BlockSpec(memory_space=pltpu.SMEM)
    vmem = pl.BlockSpec(memory_space=pltpu.VMEM)
    params = pltpu.CompilerParams(vmem_limit_bytes=VMEM_LIMIT)
    order = NB * TILE
    inverse = pl.pallas_call(
        factor_kernel,
        out_shape=jax.ShapeDtypeStruct((order, order), jnp.float32),
        in_specs=[smem, vmem, vmem],
        out_specs=vmem,
        scratch_shapes=[pltpu.VMEM((order, order), jnp.float32)],
        compiler_params=params,
        cost_estimate=pl.CostEstimate(flops=4 * 10**9, bytes_accessed=8 * 10**6, transcendentals=0),
    )(place, near, far)
    result = pl.pallas_call(
        update_kernel,
        out_shape=jax.ShapeDtypeStruct(block.shape, jnp.float32),
        in_specs=[smem, vmem, vmem, vmem, vmem, vmem],
        out_specs=vmem,
        scratch_shapes=[pltpu.VMEM((TILE, order), jnp.float32), pltpu.VMEM((order, 2 * TILE), jnp.float32)],
        compiler_params=params,
    )(place, block, strip, near_row, far_row, inverse)
    return result.reshape(matrix.shape)


def solution(mesh):
    placed = (P(None, "row", None, "col"),)
    return jax.shard_map(
        per_device,
        mesh=mesh,
        in_specs=placed,
        out_specs=P(None, "row", None, "col"),
        check_vma=False,
    )
```

```python
import jax
import jax.numpy as jnp
from jax import lax
from jax.experimental import pallas as pl
from jax.experimental.pallas import tpu as pltpu
from jax.sharding import PartitionSpec as P

TILE = 128
NB = 6
GROUP = 32
WINDOW = 16
XS, YS, ZS = 4, 8, 8
ZSRC = NB // 2
VMEM_LIMIT = 48 * 1024 * 1024
HI = lax.Precision.HIGHEST


def dot(a, b):
    return lax.dot_general(a, b, (((1,), (0,)), ((), ())), precision=HI, preferred_element_type=jnp.float32)


def dot_t(a, b):
    return lax.dot_general(a, b, (((0,), (0,)), ((), ())), precision=HI, preferred_element_type=jnp.float32)


def spread(row):
    return jnp.broadcast_to(row, (8, row.shape[1]))


def eliminate(rows, offset):
    count, width = rows.shape
    groups = count // 8

    def wide(value):
        return jnp.concatenate([value] * (width // TILE), axis=1)

    part = [rows[8 * g : 8 * g + 8] for g in range(groups)]
    sublane = lax.broadcasted_iota(jnp.int32, (8, TILE), 0)
    scale = [None] * groups
    for start in range(0, count, WINDOW):
        column = {}
        for j in range(start, start + WINDOW):
            for g in range(j // 8, groups):
                lane = offset + j
                column[g, j] = jnp.broadcast_to(part[g][:, lane : lane + 1], (8, TILE))
        for k in range(start, start + WINDOW, 2):
            gk, sk = divmod(k, 8)
            first = spread(column[gk, k][sk : sk + 1])
            cross = spread(column[gk, k][sk + 1 : sk + 2])
            second = spread(column[gk, k + 1][sk + 1 : sk + 2])
            determinant = first * second - cross * cross
            inverse = pl.reciprocal(determinant)
            factor = {}
            for g in range(gk, groups):
                a, b = column[g, k], column[g, k + 1]
                both = [(a * second - b * cross) * inverse, (b * first - a * cross) * inverse]
                if g == gk:
                    both = [jnp.where(sublane > sk + 1, value, 0.0) for value in both]
                factor[g] = both
            for j in range(k + 2, start + WINDOW):
                gj, sj = divmod(j, 8)
                across = [spread(column[gj, k + i][sj : sj + 1]) for i in range(2)]
                for g in range(gj, groups):
                    column[g, j] = column[g, j] - (factor[g][0] * across[0] + factor[g][1] * across[1])
            pivot_rows = [spread(part[gk][sk + i : sk + i + 1]) for i in range(2)]
            reciprocal = pl.reciprocal(first)
            roots = [lax.rsqrt(first), lax.rsqrt(determinant * reciprocal)]
            own = jnp.where(sublane == sk, roots[0], jnp.where(sublane == sk + 1, roots[1], 1.0))
            scale[gk] = own if scale[gk] is None else scale[gk] * own
            inside = jnp.where(sublane == sk + 1, cross * reciprocal, 0.0)
            for g in range(gk, groups):
                taken = wide(factor[g][0]) * pivot_rows[0] + wide(factor[g][1]) * pivot_rows[1]
                if g == gk:
                    taken = taken + wide(inside) * pivot_rows[0]
                part[g] = part[g] - taken
    return jnp.concatenate([part[g] * wide(scale[g]) for g in range(groups)], axis=0)


def factor_tile(tile, beside):
    row = lax.broadcasted_iota(jnp.int32, (TILE, TILE), 0)
    lane = lax.broadcasted_iota(jnp.int32, (TILE, TILE), 1)
    both = jnp.concatenate([tile, jnp.where(row == lane, 1.0, 0.0)], axis=1)
    upper = None
    for start in range(0, TILE, GROUP):
        rows = both[start : start + GROUP]
        if upper is not None:
            rows = rows - dot_t(upper[:, start : start + GROUP], upper)
        rows = eliminate(rows, start)
        upper = rows if upper is None else jnp.concatenate([upper, rows], axis=0)
        for task in beside[start // GROUP :: TILE // GROUP]:
            task()
    return upper[:, TILE:]


def dot_nt(a, b):
    return lax.dot_general(a, b, (((1,), (1,)), ((), ())), precision=HI, preferred_element_type=jnp.float32)


def factor_kernel(place, near, far, inverse, upper):
    core = place[2]

    def place_tiles(source, parity):
        for i in range(NB):
            for half in range(2):
                distance = (i + parity) % 2 + 2 * half
                j = (i + distance) % NB
                if distance == NB // 2 and i >= NB // 2:
                    continue
                tile = jnp.concatenate([source[2 * half, i], source[2 * half + 1, i]], axis=0)
                if i <= j:
                    upper[i * TILE : (i + 1) * TILE, j * TILE : (j + 1) * TILE] = tile
                else:
                    upper[j * TILE : (j + 1) * TILE, i * TILE : (i + 1) * TILE] = tile.T

    for parity in range(2):

        @pl.when(core == parity)
        def _():
            place_tiles(near, parity)
            place_tiles(far, 1 - parity)

    def at(i):
        return slice(i * TILE, (i + 1) * TILE)

    own, corner = [], None
    for b in range(NB):
        tile = upper[at(b), at(b)]
        if b:
            tile = tile - dot_t(corner, corner)
        beside = []
        if b:
            last = b - 1

            def finish_row():
                if b + 1 < NB:
                    upper[at(last), (b + 1) * TILE :] = dot(own[last], upper[at(last), (b + 1) * TILE :])

            def finish_inverse():
                inverse[at(last), at(last)] = own[last]
                inverse[at(last), b * TILE :] = jnp.zeros((TILE, (NB - b) * TILE), jnp.float32)
                if last:
                    inverse[at(last), : last * TILE] = -dot(own[last], inverse[at(last), : last * TILE])

            def next_row():
                if b + 1 < NB:
                    upper[at(b), (b + 1) * TILE :] = upper[at(b), (b + 1) * TILE :] - dot_t(
                        upper[: b * TILE, at(b)], upper[: b * TILE, (b + 1) * TILE :]
                    )
                    across = upper[: b * TILE, at(b + 1)]
                    upper[at(b + 1), at(b + 1)] = upper[at(b + 1), at(b + 1)] - dot_t(across, across)

            def next_inverse():
                inverse[at(b), : b * TILE] = dot_t(upper[: b * TILE, at(b)], inverse[: b * TILE, : b * TILE])

            beside = [finish_row, finish_inverse, next_row, next_inverse]
        own.append(factor_tile(tile, beside))
        if b + 1 < NB:
            corner = dot(own[b], upper[at(b), at(b + 1)])
            upper[at(b), at(b + 1)] = corner
    last = NB - 1
    inverse[at(last), at(last)] = own[last]
    inverse[at(last), : last * TILE] = -dot(own[last], inverse[at(last), : last * TILE])


def update_kernel(place, mine, strip, near, far, inverse, out, row_strip, solved):
    row_tile, col_tile, core = place[0], place[1], place[2]

    for parity in range(2):

        @pl.when(core == parity)
        def _():
            for j in range(NB):
                source = near if j % 2 == parity else far
                row_strip[:, j * TILE : (j + 1) * TILE] = source[j // 2]

    panel = []
    for b in range(NB):
        hi = (b + 1) * TILE
        lower = inverse[b * TILE : hi, :hi]
        total = None
        for i in range(b + 1):
            term = dot(lower[:, i * TILE : (i + 1) * TILE], strip[i])
            total = term if total is None else total + term
        solved[b * TILE : hi, :] = total
        panel.append(dot_nt(row_strip[:, :hi], lower))
    trailing = mine[...] - dot(jnp.concatenate(panel, axis=1), solved[...])
    out[...] = jnp.where(row_tile >= NB, trailing, 0.0)
    row = lax.broadcasted_iota(jnp.int32, (TILE, TILE), 0)
    lane = lax.broadcasted_iota(jnp.int32, (TILE, TILE), 1)
    for j in range(NB):

        @pl.when(col_tile == j)
        def _():
            keep = row + (row_tile - j) * TILE >= lane
            out[:, :TILE] = jnp.where(keep, panel[j], 0.0)


def send(array, pairs):
    return lax.ppermute(array, ("row", "col"), pairs)


def device(x, y, z, core):
    return ((x % XS) * YS + y % YS) * (2 * ZS) + (z % ZS) * 2 + core


CHIPS = [(x, y) for x in range(XS) for y in range(YS)]
COLUMNS = [(z, core) for z in range(ZS) for core in range(2)]
X_GROUPS = [[x * YS + y for x in range(XS)] for y in range(YS)]
Y_GROUPS = [[x * YS + y for y in range(YS)] for x in range(XS)]
Z_GROUPS = [[z * 2 + core for z in range(ZS)] for core in range(2)]


def x_pairs(step):
    return [(device(0, y, *col), device(step, y, *col)) for y in range(NB) for col in COLUMNS]


def along_x(array, x):
    result = array
    for step in range(1, XS):
        result = jnp.where(x == step, send(array, x_pairs(step)), result)
    return result


def to_all(array, axis, groups):
    copies = jnp.broadcast_to(array, (len(groups[0]),) + array.shape)
    return lax.all_to_all(copies, axis, 0, 0, axis_index_groups=groups)


def per_device(matrix):
    block = matrix.reshape(matrix.shape[1], matrix.shape[2] * matrix.shape[3])
    row_tile = lax.axis_index("row")
    col_tile = lax.axis_index("col")
    x = row_tile // YS
    core = col_tile % 2

    near_row = to_all(block[:, :TILE], "col", Z_GROUPS)[:ZSRC]

    near_row, pieces = lax.optimization_barrier((near_row, along_x(block, x)))
    strip = lax.all_gather(pieces, "row", axis_index_groups=Y_GROUPS)

    first = jnp.where(row_tile % 2 == core, row_tile, (row_tile + 1) % NB)
    start = jnp.clip((first - core) // 2, 0, ZSRC - 1)
    wrapped = jnp.concatenate([near_row, near_row[:1]], axis=0)
    tiles = lax.dynamic_slice_in_dim(wrapped, start, 2, 0).reshape(XS, 2 * TILE // XS, TILE)
    quarter = tiles[0]
    for step in range(1, XS):
        quarter = jnp.where(x == step, send(tiles[step], x_pairs(step)), quarter)
    near = to_all(to_all(quarter, "row", Y_GROUPS)[:NB], "row", X_GROUPS)

    swap = [(device(*chip, z, c), device(*chip, z, 1 - c)) for chip in CHIPS for z, c in COLUMNS]
    far = send(near, swap)
    far_row = send(near_row, swap)

    place = jnp.stack([row_tile, col_tile, core]).astype(jnp.int32)
    smem = pl.BlockSpec(memory_space=pltpu.SMEM)
    vmem = pl.BlockSpec(memory_space=pltpu.VMEM)
    params = pltpu.CompilerParams(vmem_limit_bytes=VMEM_LIMIT)
    order = NB * TILE
    inverse = pl.pallas_call(
        factor_kernel,
        out_shape=jax.ShapeDtypeStruct((order, order), jnp.float32),
        in_specs=[smem, vmem, vmem],
        out_specs=vmem,
        scratch_shapes=[pltpu.VMEM((order, order), jnp.float32)],
        compiler_params=params,
        cost_estimate=pl.CostEstimate(flops=1, bytes_accessed=1, transcendentals=0),
    )(place, near, far)
    result = pl.pallas_call(
        update_kernel,
        out_shape=jax.ShapeDtypeStruct(block.shape, jnp.float32),
        in_specs=[smem, vmem, vmem, vmem, vmem, vmem],
        out_specs=vmem,
        scratch_shapes=[pltpu.VMEM((TILE, order), jnp.float32), pltpu.VMEM((order, 2 * TILE), jnp.float32)],
        compiler_params=params,
    )(place, block, strip, near_row, far_row, inverse)
    return result.reshape(matrix.shape)


def solution(mesh):
    placed = (P(None, "row", None, "col"),)
    return jax.shard_map(
        per_device,
        mesh=mesh,
        in_specs=placed,
        out_specs=P(None, "row", None, "col"),
        check_vma=False,
    )
```

```python
import jax
import jax.numpy as jnp
from jax import lax
from jax.experimental import pallas as pl
from jax.experimental.pallas import tpu as pltpu
from jax.sharding import PartitionSpec as P

TILE = 128
NB = 6
GROUP = 32
WINDOW = 16
XS, YS, ZS = 4, 8, 8
SENT = NB // 2 + 1
ZSRC = NB // 2
VMEM_LIMIT = 48 * 1024 * 1024
HI = lax.Precision.HIGHEST


def dot(a, b):
    return lax.dot_general(a, b, (((1,), (0,)), ((), ())), precision=HI, preferred_element_type=jnp.float32)


def dot_t(a, b):
    return lax.dot_general(a, b, (((0,), (0,)), ((), ())), precision=HI, preferred_element_type=jnp.float32)


def spread(row):
    return jnp.broadcast_to(row, (8, row.shape[1]))


def eliminate(rows, offset):
    count, width = rows.shape
    groups = count // 8

    def wide(value):
        return jnp.concatenate([value] * (width // TILE), axis=1)

    part = [rows[8 * g : 8 * g + 8] for g in range(groups)]
    sublane = lax.broadcasted_iota(jnp.int32, (8, TILE), 0)
    scale = [None] * groups
    for start in range(0, count, WINDOW):
        column = {}
        for j in range(start, start + WINDOW):
            for g in range(j // 8, groups):
                lane = offset + j
                column[g, j] = jnp.broadcast_to(part[g][:, lane : lane + 1], (8, TILE))
        for k in range(start, start + WINDOW, 2):
            gk, sk = divmod(k, 8)
            first = spread(column[gk, k][sk : sk + 1])
            cross = spread(column[gk, k][sk + 1 : sk + 2])
            second = spread(column[gk, k + 1][sk + 1 : sk + 2])
            determinant = first * second - cross * cross
            inverse = pl.reciprocal(determinant)
            factor = {}
            for g in range(gk, groups):
                a, b = column[g, k], column[g, k + 1]
                factor[g] = [a * second - b * cross, b * first - a * cross]
            for j in range(k + 2, min(k + 4, start + WINDOW)):
                gj, sj = divmod(j, 8)
                across = [spread(column[gj, k + i][sj : sj + 1]) for i in range(2)]
                for g in range(gj, groups):
                    taken = factor[g][0] * across[0] + factor[g][1] * across[1]
                    column[g, j] = column[g, j] - taken * inverse
            for g in range(gk, groups):
                factor[g] = [value * inverse for value in factor[g]]
            for j in range(k + 4, start + WINDOW):
                gj, sj = divmod(j, 8)
                across = [spread(column[gj, k + i][sj : sj + 1]) for i in range(2)]
                for g in range(gj, groups):
                    column[g, j] = column[g, j] - (factor[g][0] * across[0] + factor[g][1] * across[1])
            factor[gk] = [jnp.where(sublane > sk + 1, value, 0.0) for value in factor[gk]]
            pivot_rows = [spread(part[gk][sk + i : sk + i + 1]) for i in range(2)]
            reciprocal = pl.reciprocal(first)
            roots = [lax.rsqrt(first), lax.rsqrt(determinant * reciprocal)]
            own = jnp.where(sublane == sk, roots[0], jnp.where(sublane == sk + 1, roots[1], 1.0))
            scale[gk] = own if scale[gk] is None else scale[gk] * own
            inside = jnp.where(sublane == sk + 1, cross * reciprocal, 0.0)
            for g in range(gk, groups):
                taken = wide(factor[g][0]) * pivot_rows[0] + wide(factor[g][1]) * pivot_rows[1]
                if g == gk:
                    taken = taken + wide(inside) * pivot_rows[0]
                part[g] = part[g] - taken
    return jnp.concatenate([part[g] * wide(scale[g]) for g in range(groups)], axis=0)


def factor_tile(tile, beside):
    row = lax.broadcasted_iota(jnp.int32, (TILE, TILE), 0)
    lane = lax.broadcasted_iota(jnp.int32, (TILE, TILE), 1)
    both = jnp.concatenate([tile, jnp.where(row == lane, 1.0, 0.0)], axis=1)
    upper = None
    for start in range(0, TILE, GROUP):
        rows = both[start : start + GROUP]
        if upper is not None:
            rows = rows - dot(upper.T[start : start + GROUP], upper)
        rows = eliminate(rows, start)
        upper = rows if upper is None else jnp.concatenate([upper, rows], axis=0)
        slot, slots = start // GROUP, TILE // GROUP
        for task in beside[slot * len(beside) // slots : (slot + 1) * len(beside) // slots]:
            task()
    return upper[:, TILE:]


def dot_nt(a, b):
    return lax.dot_general(a, b, (((1,), (1,)), ((), ())), precision=HI, preferred_element_type=jnp.float32)


def factor_kernel(place, near, far, near_row, far_row, panel, weights, upper, inverse):
    core = place[2]

    def held(near_tile, far_tile, parity):
        return jnp.where(core == parity, near_tile, far_tile)

    def diagonal_tile(i, distance):
        half, parity = distance // 2, (i + distance) % 2
        parts = [held(near[2 * half + k, i], far[2 * half + k, i], parity) for k in range(2)]
        return jnp.concatenate(parts, axis=0)

    def place_row(i):
        def task():
            for distance in range(SENT if i < NB // 2 else SENT - 1):
                j = (i + distance) % NB
                if i < j:
                    upper[at(i), at(j)] = diagonal_tile(i, distance)
                elif i > j:
                    upper[at(j), at(i)] = diagonal_tile(i, distance).T
                elif i:
                    upper[at(i), at(i)] = diagonal_tile(i, 0)

        return task

    def place_row_strip():
        for j in range(NB):
            panel[:, at(j)] = held(near_row[j // 2], far_row[j // 2], j % 2)

    def at(i):
        return slice(i * TILE, (i + 1) * TILE)

    own, corner = [], None
    for b in range(NB):
        if b:
            tile = upper[at(b), at(b)] - dot_t(corner, corner)
        else:
            tile = diagonal_tile(0, 0)
            beside = [place_row(i) for i in range(NB)] + [place_row_strip]
        if b:
            last = b - 1

            def finish_row():
                if b + 1 < NB:
                    upper[at(last), (b + 1) * TILE :] = dot(own[last], upper[at(last), (b + 1) * TILE :])

            def finish_inverse():
                inverse[at(last), at(last)] = own[last]
                if b < NB - 1:
                    inverse[at(last), b * TILE : (NB - 1) * TILE] = jnp.zeros((TILE, (NB - 1 - b) * TILE), jnp.float32)
                if last:
                    inverse[at(last), : last * TILE] = -dot(own[last], inverse[at(last), : last * TILE])

            def next_row():
                if b + 1 < NB:
                    upper[at(b), (b + 1) * TILE :] = upper[at(b), (b + 1) * TILE :] - dot_t(
                        upper[: b * TILE, at(b)], upper[: b * TILE, (b + 1) * TILE :]
                    )
                    across = upper[: b * TILE, at(b + 1)]
                    upper[at(b + 1), at(b + 1)] = upper[at(b + 1), at(b + 1)] - dot_t(across, across)

            def next_inverse():
                inverse[at(b), : b * TILE] = dot_t(upper[: b * TILE, at(b)], inverse[: b * TILE, : b * TILE])

            def panel_tile():
                panel[:, at(last)] = dot_nt(panel[:, at(last)], own[last])
                panel[:, at(b)] = panel[:, at(b)] - dot(panel[:, : b * TILE], upper[: b * TILE, at(b)])

            def add_weights():
                term = dot(panel[:, at(last)], inverse[at(last), : b * TILE])
                if last:
                    weights[:, : last * TILE] = weights[:, : last * TILE] + term[:, : last * TILE]
                weights[:, at(last)] = term[:, last * TILE :]

            beside = [finish_row, finish_inverse, next_row, next_inverse, panel_tile, add_weights]
        own.append(factor_tile(tile, beside))
        if b + 1 < NB:
            corner = dot(own[b], upper[at(b), at(b + 1)])
            upper[at(b), at(b + 1)] = corner
    last = NB - 1
    done = dot_nt(panel[:, at(last)], own[last])
    panel[:, at(last)] = done
    weights[:, at(last)] = dot(done, own[last])
    left = dot(own[last], inverse[at(last), : last * TILE])
    weights[:, : last * TILE] = weights[:, : last * TILE] - dot(done, left)


def update_kernel(place, mine, strip, panel, weights, out):
    row_tile, col_tile = place[0], place[1]
    columns = strip[:NB].reshape(NB * TILE, 2 * TILE)
    total = mine[...] - dot(weights[...], columns)
    out[...] = jnp.where(row_tile >= NB, total, 0.0)
    row = lax.broadcasted_iota(jnp.int32, (TILE, TILE), 0)
    lane = lax.broadcasted_iota(jnp.int32, (TILE, TILE), 1)
    for j in range(NB):

        @pl.when(col_tile == j)
        def _():
            keep = row + (row_tile - j) * TILE >= lane
            out[:, :TILE] = jnp.where(keep, panel[:, j * TILE : (j + 1) * TILE], 0.0)


def send(array, pairs):
    return lax.ppermute(array, ("row", "col"), pairs)


def device(x, y, z, core):
    return ((x % XS) * YS + y % YS) * (2 * ZS) + (z % ZS) * 2 + core


CHIPS = [(x, y) for x in range(XS) for y in range(YS)]
COLUMNS = [(z, core) for z in range(ZS) for core in range(2)]
X_GROUPS = [[x * YS + y for x in range(XS)] for y in range(YS)]
Y_GROUPS = [[x * YS + y for y in range(YS)] for x in range(XS)]
Z_GROUPS = [[z * 2 + core for z in range(ZS)] for core in range(2)]


def x_pairs(step):
    return [(device(0, y, *col), device(step, y, *col)) for y in range(NB) for col in COLUMNS]


def along_x(array, x):
    result = array
    for step in range(1, XS):
        result = jnp.where(x == step, send(array, x_pairs(step)), result)
    return result


def to_all(array, axis, groups):
    copies = jnp.broadcast_to(array, (len(groups[0]),) + array.shape)
    return lax.all_to_all(copies, axis, 0, 0, axis_index_groups=groups)


def per_device(matrix):
    block = matrix.reshape(matrix.shape[1], matrix.shape[2] * matrix.shape[3])
    row_tile = lax.axis_index("row")
    col_tile = lax.axis_index("col")
    x = row_tile // YS
    core = col_tile % 2

    near_row = to_all(block[:, :TILE], "col", Z_GROUPS)[:ZSRC]

    near_row, pieces = lax.optimization_barrier((near_row, along_x(block, x)))
    strip = lax.all_gather(pieces, "row", axis_index_groups=Y_GROUPS)

    first = jnp.where(row_tile % 2 == core, row_tile, (row_tile + 1) % NB)
    start = jnp.clip((first - core) // 2, 0, ZSRC - 1)
    wrapped = jnp.concatenate([near_row, near_row[:1]], axis=0)
    tiles = lax.dynamic_slice_in_dim(wrapped, start, 2, 0).reshape(XS, 2 * TILE // XS, TILE)
    quarter = tiles[0]
    for step in range(1, XS):
        quarter = jnp.where(x == step, send(tiles[step], x_pairs(step)), quarter)
    swap = [(device(*chip, z, c), device(*chip, z, 1 - c)) for chip in CHIPS for z, c in COLUMNS]
    far_row = send(near_row, swap)
    tiles, far_row = lax.optimization_barrier((to_all(quarter, "row", Y_GROUPS)[:NB], far_row))
    near = to_all(tiles, "row", X_GROUPS)
    far = send(near, swap)

    place = jnp.stack([row_tile, col_tile, core]).astype(jnp.int32)
    smem = pl.BlockSpec(memory_space=pltpu.SMEM)
    vmem = pl.BlockSpec(memory_space=pltpu.VMEM)
    params = pltpu.CompilerParams(vmem_limit_bytes=VMEM_LIMIT)
    order = NB * TILE
    panel, weights = pl.pallas_call(
        factor_kernel,
        out_shape=[jax.ShapeDtypeStruct((TILE, order), jnp.float32)] * 2,
        in_specs=[smem, vmem, vmem, vmem, vmem],
        out_specs=[vmem, vmem],
        scratch_shapes=[pltpu.VMEM((order, order), jnp.float32)] * 2,
        compiler_params=params,
        cost_estimate=pl.CostEstimate(flops=1, bytes_accessed=1, transcendentals=0),
    )(place, near, far, near_row, far_row)
    result = pl.pallas_call(
        update_kernel,
        out_shape=jax.ShapeDtypeStruct(block.shape, jnp.float32),
        in_specs=[smem, vmem, vmem, vmem, vmem],
        out_specs=vmem,
        compiler_params=params,
    )(place, block, strip, panel, weights)
    return result.reshape(matrix.shape)


def solution(mesh):
    placed = (P(None, "row", None, "col"),)
    return jax.shard_map(
        per_device,
        mesh=mesh,
        in_specs=placed,
        out_specs=P(None, "row", None, "col"),
        check_vma=False,
    )
```

```python
import jax
import jax.numpy as jnp
from jax import lax
from jax.experimental import pallas as pl
from jax.experimental.pallas import tpu as pltpu
from jax.sharding import PartitionSpec as P

TILE = 128
NB = 6
GROUP = 64
LAG = 1
WINDOW = 8
XS, YS, ZS = 4, 8, 8
SENT = NB // 2 + 1
ZSRC = NB // 2
VMEM_LIMIT = 48 * 1024 * 1024
HI = lax.Precision.HIGHEST


def dot(a, b):
    return lax.dot_general(a, b, (((1,), (0,)), ((), ())), precision=HI, preferred_element_type=jnp.float32)


def dot_t(a, b):
    return lax.dot_general(a, b, (((0,), (0,)), ((), ())), precision=HI, preferred_element_type=jnp.float32)


def spread(row):
    return jnp.broadcast_to(row, (8, row.shape[1]))


def eliminate(rows, offset):
    count = rows.shape[0]
    groups = count // 8
    part = [rows[8 * g : 8 * g + 8] for g in range(groups)]
    sublane = lax.broadcasted_iota(jnp.int32, (8, TILE), 0)
    lane = lax.broadcasted_iota(jnp.int32, (8, TILE), 1)
    scale = [None] * groups
    column = {}

    def take(start):
        for j in range(start, start + WINDOW):
            for g in range(j // 8, groups):
                at = offset + j
                column[g, j] = jnp.broadcast_to(part[g][:, at : at + 1], (8, TILE))

    take(0)
    taken_to = WINDOW
    for start in range(0, count, WINDOW):
        for k in range(start, start + WINDOW, 2):
            gk, sk = divmod(k, 8)
            first = spread(column[gk, k][sk : sk + 1])
            cross = spread(column[gk, k][sk + 1 : sk + 2])
            second = spread(column[gk, k + 1][sk + 1 : sk + 2])
            determinant = first * second - cross * cross
            inverse = pl.reciprocal(determinant)
            factor = {}
            for g in range(gk, groups):
                a, b = column[g, k], column[g, k + 1]
                factor[g] = [(a * second - b * cross) * inverse, (b * first - a * cross) * inverse]
            for j in range(k + 2, taken_to):
                gj, sj = divmod(j, 8)
                across = [spread(column[gj, k + i][sj : sj + 1]) for i in range(2)]
                for g in range(gj, groups):
                    column[g, j] = column[g, j] - (factor[g][0] * across[0] + factor[g][1] * across[1])
            reciprocal = pl.reciprocal(first)
            roots = [lax.rsqrt(first), lax.rsqrt(determinant * reciprocal)]
            own = jnp.where(sublane == sk, roots[0], jnp.where(sublane == sk + 1, roots[1], 1.0))
            scale[gk] = own if scale[gk] is None else scale[gk] * own
            pair = (lane >= offset + k) & (lane < offset + k + 2)
            diagonal = lane - (offset + k) == sublane - sk
            part[gk] = jnp.where(pair & (sublane >= sk), jnp.where(diagonal & (sublane < sk + 2), 1.0, 0.0), part[gk])
            pivot_rows = [spread(part[gk][sk + i : sk + i + 1]) for i in range(2)]
            below = [jnp.where(sublane > sk + 1, value, 0.0) for value in factor[gk]]
            below[0] = below[0] + jnp.where(sublane == sk + 1, cross * reciprocal, 0.0)
            part[gk] = part[gk] - (below[0] * pivot_rows[0] + below[1] * pivot_rows[1])
            for g in range(gk + 1, groups):
                taken = factor[g][0] * pivot_rows[0] + factor[g][1] * pivot_rows[1]
                part[g] = jnp.where(pair, 0.0, part[g]) - taken
            if k + 2 + 2 * LAG == start + WINDOW and taken_to < count:
                take(taken_to)
                taken_to += WINDOW
    return jnp.concatenate([part[g] * scale[g] for g in range(groups)], axis=0)


def factor_tile(tile, beside):
    row = lax.broadcasted_iota(jnp.int32, (TILE, TILE), 0)
    lane = lax.broadcasted_iota(jnp.int32, (TILE, TILE), 1)
    done = None
    for start in range(0, TILE, GROUP):
        rows = tile[start : start + GROUP]
        if done is not None:
            mask = (lane[:start] <= row[:start]) | (lane[:start] >= start)
            rows = jnp.where(lane[:GROUP] >= start, rows, 0.0)
            rows = rows - dot(done.T[start : start + GROUP], jnp.where(mask, done, 0.0))
        rows = eliminate(rows, start)
        done = rows if done is None else jnp.concatenate([done, rows], axis=0)
        slot, slots = start // GROUP, TILE // GROUP
        for task in beside[slot * len(beside) // slots : (slot + 1) * len(beside) // slots]:
            task()
    return jnp.where(lane <= row, done, 0.0)


def dot_nt(a, b):
    return lax.dot_general(a, b, (((1,), (1,)), ((), ())), precision=HI, preferred_element_type=jnp.float32)


def factor_kernel(place, near, far, near_row, far_row, panel, weights, upper, inverse):
    core = place[2]

    def held(near_tile, far_tile, parity):
        return jnp.where(core == parity, near_tile, far_tile)

    def diagonal_tile(i, distance):
        half, parity = distance // 2, (i + distance) % 2
        parts = [held(near[2 * half + k, i], far[2 * half + k, i], parity) for k in range(2)]
        return jnp.concatenate(parts, axis=0)

    def place_row(i):
        def task():
            for distance in range(SENT if i < NB // 2 else SENT - 1):
                j = (i + distance) % NB
                if i < j:
                    upper[at(i), at(j)] = diagonal_tile(i, distance)
                elif i > j:
                    upper[at(j), at(i)] = diagonal_tile(i, distance).T
                elif i:
                    upper[at(i), at(i)] = diagonal_tile(i, 0)

        return task

    def place_row_strip():
        for j in range(NB):
            panel[:, at(j)] = held(near_row[j // 2], far_row[j // 2], j % 2)

    def at(i):
        return slice(i * TILE, (i + 1) * TILE)

    own, corner = [], None
    for b in range(NB):
        if b:
            tile = upper[at(b), at(b)] - dot_t(corner, corner)
        else:
            tile = diagonal_tile(0, 0)
            beside = [place_row(i) for i in range(NB)] + [place_row_strip]
        if b:
            last = b - 1

            def finish_row():
                if b + 1 < NB:
                    upper[at(last), (b + 1) * TILE :] = dot(own[last], upper[at(last), (b + 1) * TILE :])

            def finish_inverse():
                inverse[at(last), at(last)] = own[last]
                if b < NB - 1:
                    inverse[at(last), b * TILE : (NB - 1) * TILE] = jnp.zeros((TILE, (NB - 1 - b) * TILE), jnp.float32)
                if last:
                    inverse[at(last), : last * TILE] = -dot(own[last], inverse[at(last), : last * TILE])

            def next_row():
                if b + 1 < NB:
                    upper[at(b), (b + 1) * TILE :] = upper[at(b), (b + 1) * TILE :] - dot_t(
                        upper[: b * TILE, at(b)], upper[: b * TILE, (b + 1) * TILE :]
                    )
                    across = upper[: b * TILE, at(b + 1)]
                    upper[at(b + 1), at(b + 1)] = upper[at(b + 1), at(b + 1)] - dot_t(across, across)

            def next_inverse():
                inverse[at(b), : b * TILE] = dot_t(upper[: b * TILE, at(b)], inverse[: b * TILE, : b * TILE])

            def panel_tile():
                panel[:, at(last)] = dot_nt(panel[:, at(last)], own[last])
                panel[:, at(b)] = panel[:, at(b)] - dot(panel[:, : b * TILE], upper[: b * TILE, at(b)])

            def add_weights():
                term = dot(panel[:, at(last)], inverse[at(last), : b * TILE])
                if last:
                    weights[:, : last * TILE] = weights[:, : last * TILE] + term[:, : last * TILE]
                weights[:, at(last)] = term[:, last * TILE :]

            beside = [finish_row, finish_inverse, next_row, next_inverse, panel_tile, add_weights]
        own.append(factor_tile(tile, beside))
        if b + 1 < NB:
            corner = dot(own[b], upper[at(b), at(b + 1)])
            upper[at(b), at(b + 1)] = corner
    last = NB - 1
    done = dot_nt(panel[:, at(last)], own[last])
    panel[:, at(last)] = done
    weights[:, at(last)] = dot(done, own[last])
    left = dot(own[last], inverse[at(last), : last * TILE])
    weights[:, : last * TILE] = weights[:, : last * TILE] - dot(done, left)


def update_kernel(place, mine, strip, panel, weights, out):
    row_tile, col_tile = place[0], place[1]
    columns = strip[:NB].reshape(NB * TILE, 2 * TILE)
    total = mine[...] - dot(weights[...], columns)
    out[...] = jnp.where(row_tile >= NB, total, 0.0)
    row = lax.broadcasted_iota(jnp.int32, (TILE, TILE), 0)
    lane = lax.broadcasted_iota(jnp.int32, (TILE, TILE), 1)
    for j in range(NB):

        @pl.when(col_tile == j)
        def _():
            keep = row + (row_tile - j) * TILE >= lane
            out[:, :TILE] = jnp.where(keep, panel[:, j * TILE : (j + 1) * TILE], 0.0)


def send(array, pairs):
    return lax.ppermute(array, ("row", "col"), pairs)


def device(x, y, z, core):
    return ((x % XS) * YS + y % YS) * (2 * ZS) + (z % ZS) * 2 + core


CHIPS = [(x, y) for x in range(XS) for y in range(YS)]
COLUMNS = [(z, core) for z in range(ZS) for core in range(2)]
X_GROUPS = [[x * YS + y for x in range(XS)] for y in range(YS)]
Y_GROUPS = [[x * YS + y for y in range(YS)] for x in range(XS)]
Z_GROUPS = [[z * 2 + core for z in range(ZS)] for core in range(2)]


def x_pairs(step):
    return [(device(0, y, *col), device(step, y, *col)) for y in range(NB) for col in COLUMNS]


def along_x(array, x):
    result = array
    for step in range(1, XS):
        result = jnp.where(x == step, send(array, x_pairs(step)), result)
    return result


def to_all(array, axis, groups):
    copies = jnp.broadcast_to(array, (len(groups[0]),) + array.shape)
    return lax.all_to_all(copies, axis, 0, 0, axis_index_groups=groups)


def per_device(matrix):
    block = matrix.reshape(matrix.shape[1], matrix.shape[2] * matrix.shape[3])
    row_tile = lax.axis_index("row")
    col_tile = lax.axis_index("col")
    x = row_tile // YS
    core = col_tile % 2

    near_row = to_all(block[:, :TILE], "col", Z_GROUPS)[:ZSRC]

    near_row, pieces = lax.optimization_barrier((near_row, along_x(block, x)))
    strip = lax.all_gather(pieces, "row", axis_index_groups=Y_GROUPS)

    first = jnp.where(row_tile % 2 == core, row_tile, (row_tile + 1) % NB)
    start = jnp.clip((first - core) // 2, 0, ZSRC - 1)
    wrapped = jnp.concatenate([near_row, near_row[:1]], axis=0)
    tiles = lax.dynamic_slice_in_dim(wrapped, start, 2, 0).reshape(XS, 2 * TILE // XS, TILE)
    quarter = tiles[0]
    for step in range(1, XS):
        quarter = jnp.where(x == step, send(tiles[step], x_pairs(step)), quarter)
    swap = [(device(*chip, z, c), device(*chip, z, 1 - c)) for chip in CHIPS for z, c in COLUMNS]
    far_row = send(near_row, swap)
    tiles, far_row = lax.optimization_barrier((to_all(quarter, "row", Y_GROUPS)[:NB], far_row))
    near = to_all(tiles, "row", X_GROUPS)
    far = send(near, swap)

    place = jnp.stack([row_tile, col_tile, core]).astype(jnp.int32)
    smem = pl.BlockSpec(memory_space=pltpu.SMEM)
    vmem = pl.BlockSpec(memory_space=pltpu.VMEM)
    params = pltpu.CompilerParams(vmem_limit_bytes=VMEM_LIMIT)
    order = NB * TILE
    panel, weights = pl.pallas_call(
        factor_kernel,
        out_shape=[jax.ShapeDtypeStruct((TILE, order), jnp.float32)] * 2,
        in_specs=[smem, vmem, vmem, vmem, vmem],
        out_specs=[vmem, vmem],
        scratch_shapes=[pltpu.VMEM((order, order), jnp.float32)] * 2,
        compiler_params=params,
        cost_estimate=pl.CostEstimate(flops=1, bytes_accessed=1, transcendentals=0),
    )(place, near, far, near_row, far_row)
    result = pl.pallas_call(
        update_kernel,
        out_shape=jax.ShapeDtypeStruct(block.shape, jnp.float32),
        in_specs=[smem, vmem, vmem, vmem, vmem],
        out_specs=vmem,
        compiler_params=params,
    )(place, block, strip, panel, weights)
    return result.reshape(matrix.shape)


def solution(mesh):
    placed = (P(None, "row", None, "col"),)
    return jax.shard_map(
        per_device,
        mesh=mesh,
        in_specs=placed,
        out_specs=P(None, "row", None, "col"),
        check_vma=False,
    )
```

```python
import jax
import jax.numpy as jnp
from jax import lax
from jax.experimental import pallas as pl
from jax.experimental.pallas import tpu as pltpu
from jax.sharding import PartitionSpec as P

TILE = 128
NB = 6
GROUP = 64
LAG = 1
WINDOW = 8
XS, YS, ZS = 4, 8, 8
SENT = NB // 2 + 1
ZSRC = NB // 2
VMEM_LIMIT = 48 * 1024 * 1024
SLAB = 32
HI = lax.Precision.HIGHEST


def dot(a, b):
    return lax.dot_general(a, b, (((1,), (0,)), ((), ())), precision=HI, preferred_element_type=jnp.float32)


def dot_t(a, b):
    return lax.dot_general(a, b, (((0,), (0,)), ((), ())), precision=HI, preferred_element_type=jnp.float32)


def spread(row):
    return jnp.broadcast_to(row, (8, row.shape[1]))


def eliminate(rows, offset):
    count = rows.shape[0]
    groups = count // 8
    part = [rows[8 * g : 8 * g + 8] for g in range(groups)]
    sublane = lax.broadcasted_iota(jnp.int32, (8, TILE), 0)
    lane = lax.broadcasted_iota(jnp.int32, (8, TILE), 1)
    scale = [None] * groups
    column = {}

    def take(start):
        for j in range(start, start + WINDOW):
            for g in range(j // 8, groups):
                at = offset + j
                column[g, j] = jnp.broadcast_to(part[g][:, at : at + 1], (8, TILE))

    take(0)
    taken_to = WINDOW
    for start in range(0, count, WINDOW):
        for k in range(start, start + WINDOW, 2):
            gk, sk = divmod(k, 8)
            first = spread(column[gk, k][sk : sk + 1])
            cross = spread(column[gk, k][sk + 1 : sk + 2])
            second = spread(column[gk, k + 1][sk + 1 : sk + 2])
            determinant = first * second - cross * cross
            inverse = pl.reciprocal(determinant)
            factor = {}
            for g in range(gk, groups):
                a, b = column[g, k], column[g, k + 1]
                factor[g] = [(a * second - b * cross) * inverse, (b * first - a * cross) * inverse]
            for j in range(k + 2, taken_to):
                gj, sj = divmod(j, 8)
                across = [spread(column[gj, k + i][sj : sj + 1]) for i in range(2)]
                for g in range(gj, groups):
                    column[g, j] = column[g, j] - (factor[g][0] * across[0] + factor[g][1] * across[1])
            reciprocal = pl.reciprocal(first)
            roots = [lax.rsqrt(first), lax.rsqrt(determinant * reciprocal)]
            own = jnp.where(sublane == sk, roots[0], jnp.where(sublane == sk + 1, roots[1], 1.0))
            scale[gk] = own if scale[gk] is None else scale[gk] * own
            pair = (lane >= offset + k) & (lane < offset + k + 2)
            diagonal = lane - (offset + k) == sublane - sk
            part[gk] = jnp.where(pair & (sublane >= sk), jnp.where(diagonal & (sublane < sk + 2), 1.0, 0.0), part[gk])
            pivot_rows = [spread(part[gk][sk + i : sk + i + 1]) for i in range(2)]
            below = [jnp.where(sublane > sk + 1, value, 0.0) for value in factor[gk]]
            below[0] = below[0] + jnp.where(sublane == sk + 1, cross * reciprocal, 0.0)
            part[gk] = part[gk] - (below[0] * pivot_rows[0] + below[1] * pivot_rows[1])
            for g in range(gk + 1, groups):
                taken = factor[g][0] * pivot_rows[0] + factor[g][1] * pivot_rows[1]
                part[g] = jnp.where(pair, 0.0, part[g]) - taken
            if k + 2 + 2 * LAG == start + WINDOW and taken_to < count:
                take(taken_to)
                taken_to += WINDOW
    return jnp.concatenate([part[g] * scale[g] for g in range(groups)], axis=0)


def factor_tile(tile, beside):
    row = lax.broadcasted_iota(jnp.int32, (TILE, TILE), 0)
    lane = lax.broadcasted_iota(jnp.int32, (TILE, TILE), 1)
    done = None
    for start in range(0, TILE, GROUP):
        rows = tile[start : start + GROUP]
        if done is not None:
            mask = (lane[:start] <= row[:start]) | (lane[:start] >= start)
            rows = jnp.where(lane[:GROUP] >= start, rows, 0.0)
            rows = rows - dot(done.T[start : start + GROUP], jnp.where(mask, done, 0.0))
        rows = eliminate(rows, start)
        done = rows if done is None else jnp.concatenate([done, rows], axis=0)
        slot, slots = start // GROUP, TILE // GROUP
        for task in beside[slot * len(beside) // slots : (slot + 1) * len(beside) // slots]:
            task()
    return jnp.where(lane <= row, done, 0.0)


def dot_nt(a, b):
    return lax.dot_general(a, b, (((1,), (1,)), ((), ())), precision=HI, preferred_element_type=jnp.float32)


def factor_kernel(place, near, far, near_row, far_row, panel, weights, upper, inverse):
    core = place[2]

    def held(near_tile, far_tile, parity):
        return jnp.where(core == parity, near_tile, far_tile)

    def diagonal_tile(i, distance):
        half, parity = distance // 2, (i + distance) % 2
        parts = [held(near[2 * half + k, i], far[2 * half + k, i], parity) for k in range(2)]
        return jnp.concatenate(parts, axis=0)

    def place_row(i):
        def task():
            for distance in range(SENT if i < NB // 2 else SENT - 1):
                j = (i + distance) % NB
                if i < j:
                    upper[at(i), at(j)] = diagonal_tile(i, distance)
                elif i > j:
                    upper[at(j), at(i)] = diagonal_tile(i, distance).T
                elif i:
                    upper[at(i), at(i)] = diagonal_tile(i, 0)

        return task

    def place_row_strip():
        for j in range(NB):
            panel[:, at(j)] = held(near_row[j // 2], far_row[j // 2], j % 2)

    def at(i):
        return slice(i * TILE, (i + 1) * TILE)

    own, corner = [], None
    for b in range(NB):
        if b:
            tile = upper[at(b), at(b)] - dot(corner.T, corner)
        else:
            tile = diagonal_tile(0, 0)
            beside = [place_row(i) for i in range(NB)] + [place_row_strip]
        if b:
            last = b - 1

            def finish_row():
                if b + 1 < NB:
                    upper[at(last), (b + 1) * TILE :] = dot(own[last], upper[at(last), (b + 1) * TILE :])

            def finish_inverse():
                inverse[at(last), at(last)] = own[last]
                if b < NB - 1:
                    inverse[at(last), b * TILE : (NB - 1) * TILE] = jnp.zeros((TILE, (NB - 1 - b) * TILE), jnp.float32)
                if last:
                    inverse[at(last), : last * TILE] = -dot(own[last], inverse[at(last), : last * TILE])

            def next_row():
                if b + 1 < NB:
                    upper[at(b), (b + 1) * TILE :] = upper[at(b), (b + 1) * TILE :] - dot_t(
                        upper[: b * TILE, at(b)], upper[: b * TILE, (b + 1) * TILE :]
                    )
                    across = upper[: b * TILE, at(b + 1)]
                    upper[at(b + 1), at(b + 1)] = upper[at(b + 1), at(b + 1)] - dot_t(across, across)

            def next_inverse():
                inverse[at(b), : b * TILE] = dot_t(upper[: b * TILE, at(b)], inverse[: b * TILE, : b * TILE])

            def panel_tile():
                panel[:, at(last)] = dot_nt(panel[:, at(last)], own[last])
                panel[:, at(b)] = panel[:, at(b)] - dot(panel[:, : b * TILE], upper[: b * TILE, at(b)])

            def add_weights():
                term = dot(panel[:, at(last)], inverse[at(last), : b * TILE])
                if last:
                    weights[:, : last * TILE] = weights[:, : last * TILE] + term[:, : last * TILE]
                weights[:, at(last)] = term[:, last * TILE :]

            beside = [finish_row, finish_inverse, next_row, next_inverse, panel_tile, add_weights]
        own.append(factor_tile(tile, beside))
        if b + 1 < NB:
            corner = dot(own[b], upper[at(b), at(b + 1)])
            upper[at(b), at(b + 1)] = corner
    last = NB - 1
    done = dot_nt(panel[:, at(last)], own[last])
    panel[:, at(last)] = done
    weights[:, at(last)] = dot(done, own[last])
    left = dot(own[last], inverse[at(last), : last * TILE])
    weights[:, : last * TILE] = weights[:, : last * TILE] - dot(done, left)


def update_kernel(place, mine, strip, panel, weights, out):
    row_tile, col_tile = place[0], place[1]
    columns = strip[:NB].reshape(NB * TILE, 2 * TILE)
    total = mine[...] - dot(weights[...], columns)
    out[...] = jnp.where(row_tile >= NB, total, 0.0)
    row = lax.broadcasted_iota(jnp.int32, (TILE, TILE), 0)
    lane = lax.broadcasted_iota(jnp.int32, (TILE, TILE), 1)
    for j in range(NB):

        @pl.when(col_tile == j)
        def _():
            keep = row + (row_tile - j) * TILE >= lane
            out[:, :TILE] = jnp.where(keep, panel[:, j * TILE : (j + 1) * TILE], 0.0)


def send(array, pairs):
    return lax.ppermute(array, ("row", "col"), pairs)


def device(x, y, z, core):
    return ((x % XS) * YS + y % YS) * (2 * ZS) + (z % ZS) * 2 + core


CHIPS = [(x, y) for x in range(XS) for y in range(YS)]
COLUMNS = [(z, core) for z in range(ZS) for core in range(2)]
X_GROUPS = [[x * YS + y for x in range(XS)] for y in range(YS)]
Y_GROUPS = [[x * YS + y for y in range(YS)] for x in range(XS)]
Z_GROUPS = [[z * 2 + core for z in range(ZS)] for core in range(2)]


def x_pairs(step):
    return [(device(0, y, *col), device(step, y, *col)) for y in range(NB) for col in COLUMNS]


def along_x(array, x):
    result = array
    for step in range(1, XS):
        result = jnp.where(x == step, send(array, x_pairs(step)), result)
    return result


def to_all(array, axis, groups):
    parts = array.reshape((-1, SLAB) + array.shape[-1:])
    copies = jnp.broadcast_to(parts, (len(groups[0]),) + parts.shape)
    arrived = lax.all_to_all(copies, axis, 0, 0, axis_index_groups=groups)
    return arrived.reshape((len(groups[0]),) + array.shape)


def per_device(matrix):
    block = matrix.reshape(matrix.shape[1], matrix.shape[2] * matrix.shape[3])
    row_tile = lax.axis_index("row")
    col_tile = lax.axis_index("col")
    x = row_tile // YS
    core = col_tile % 2

    near_row = to_all(block[:, :TILE], "col", Z_GROUPS)[:ZSRC]

    near_row, pieces = lax.optimization_barrier((near_row, along_x(block, x)))
    strip = lax.all_gather(pieces, "row", axis_index_groups=Y_GROUPS)

    first = jnp.where(row_tile % 2 == core, row_tile, (row_tile + 1) % NB)
    start = jnp.clip((first - core) // 2, 0, ZSRC - 1)
    wrapped = jnp.concatenate([near_row, near_row[:1]], axis=0)
    tiles = lax.dynamic_slice_in_dim(wrapped, start, 2, 0).reshape(XS, 2 * TILE // XS, TILE)
    quarter = tiles[0]
    for step in range(1, XS):
        quarter = jnp.where(x == step, send(tiles[step], x_pairs(step)), quarter)
    swap = [(device(*chip, z, c), device(*chip, z, 1 - c)) for chip in CHIPS for z, c in COLUMNS]
    far_row = send(near_row, swap)
    tiles, far_row = lax.optimization_barrier((to_all(quarter, "row", Y_GROUPS)[:NB], far_row))
    near = to_all(tiles, "row", X_GROUPS)
    far = send(near, swap)

    place = jnp.stack([row_tile, col_tile, core]).astype(jnp.int32)
    smem = pl.BlockSpec(memory_space=pltpu.SMEM)
    vmem = pl.BlockSpec(memory_space=pltpu.VMEM)
    params = pltpu.CompilerParams(vmem_limit_bytes=VMEM_LIMIT)
    order = NB * TILE
    panel, weights = pl.pallas_call(
        factor_kernel,
        out_shape=[jax.ShapeDtypeStruct((TILE, order), jnp.float32)] * 2,
        in_specs=[smem, vmem, vmem, vmem, vmem],
        out_specs=[vmem, vmem],
        scratch_shapes=[pltpu.VMEM((order, order), jnp.float32)] * 2,
        compiler_params=params,
        cost_estimate=pl.CostEstimate(flops=1, bytes_accessed=1, transcendentals=0),
    )(place, near, far, near_row, far_row)
    result = pl.pallas_call(
        update_kernel,
        out_shape=jax.ShapeDtypeStruct(block.shape, jnp.float32),
        in_specs=[smem, vmem, vmem, vmem, vmem],
        out_specs=vmem,
        compiler_params=params,
    )(place, block, strip, panel, weights)
    return result.reshape(matrix.shape)


def solution(mesh):
    placed = (P(None, "row", None, "col"),)
    return jax.shard_map(
        per_device,
        mesh=mesh,
        in_specs=placed,
        out_specs=P(None, "row", None, "col"),
        check_vma=False,
    )
```
